32 devices in a mesh: day: 4 (over y, x), lon: 4 (over z), lat: 2 (over core).
Axes of the slice: x: 2, y: 2, z: 4, core: 2. Of those that a mesh axis runs over, the one named last changes fastest.
Arguments:
- historical_runs: bfloat16 [64, 5, 3, 180, 256], P('day', None, None, 'lon', 'lat'), may hold values from -6 to 6
- todays_outlook: bfloat16 [5, 3, 180, 256], P(None, None, 'lon', 'lat'), may hold values from -6 to 6
- variable_importance: float32 [5], replicated, may hold values from 0.3 to 3
- verifying_measurements: bfloat16 [64, 3, 180, 256], P('day', None, 'lon', 'lat'), may hold values from -6 to 6
- matching_dates_chosen: int32 [3, 180, 256, 20], P(None, 'lon', ('lat', 'day')), may hold values from 0 to 63, all different within a row
Outputs:
- metric: float32 [64, 3, 180, 256], P('day', None, 'lon', 'lat')
- prediction: float32 [3, 180, 256], P(None, 'lon', ('lat', 'day'))
The draws below stay inside these ranges and needn't reach their ends.
Inputs may be any that keep to these rules, and one draw needn't show every extreme that they name: `matching_dates_chosen`: each cell and lead names 20 different days.
All inputs are finite; a program needn't handle non-finite values.
Results may differ from the reference program's by a relative error of at most 0.0028.
Values may be sent and summed in bfloat16 or wider, within the bound.
A program may use at most 64 MiB of HBM per device.

```python
import math
import jax
import jax.numpy as jnp
from jax import lax

INPUT_VARIABLES = 5
HORIZON_STEPS = 3
MATCH_NUMBER = 20
ARCHIVE_DATES = 64
EAST_WEST_BINS = 180
NORTH_SOUTH_BINS = 256


def steps_of(own_key, dims, shards, least, high):
    def one(axis_at, blocks):
        heights = jax.random.uniform(jax.random.fold_in(jax.random.fold_in(own_key, 6), axis_at), (blocks,), jnp.float32, least / len(shards), high / len(shards))
        return jnp.repeat(jnp.exp(heights), dims[axis_at] // blocks).reshape((-1,) + (1,) * (len(dims) - axis_at - 1))

    factor_of = one(*shards[0])
    for cut in shards[1:]:
        factor_of = factor_of * one(*cut)
    return factor_of


def different_ones(key, rows, number_of, top, lift):
    ranking = jax.random.permutation(jax.random.fold_in(key, 1), number_of)
    boost = ranking
    for power in range(3):
        boost = boost * boost // number_of
    boost = boost * lift // number_of
    tickets = jax.random.randint(jax.random.fold_in(key, 2), (rows, number_of), 0, 4096) + boost
    fixed_rows = jax.random.permutation(jax.random.fold_in(key, 3), rows)[jnp.arange(number_of) % rows]
    tickets = jnp.where(jnp.arange(rows)[:, None] == fixed_rows[None, :], 1 << 14, tickets)
    priority = tickets * number_of + jnp.arange(number_of)
    return lax.top_k(priority.astype(jnp.int32), top)[1].astype(jnp.int32)


def noise(rng, shape, spread, bound, pieces=(), held_as=jnp.bfloat16):
    array = jax.random.normal(rng, shape, jnp.float32) * spread
    if len(pieces) > 0:
        array = steps_of(rng, shape, pieces, -0.22, 0.18) * array
    return jnp.clip(array, min=-bound, max=bound).astype(held_as)


def setup_inputs(seed: int = 0) -> dict:
    keys = jax.random.split(jax.random.key(seed), 6)
    return {
        "historical_runs": noise(keys[0], (ARCHIVE_DATES, INPUT_VARIABLES, HORIZON_STEPS, EAST_WEST_BINS, NORTH_SOUTH_BINS), 1.0, 6.0, ((0, 4), (3, 4), (4, 2))),
        "todays_outlook": noise(keys[1], (INPUT_VARIABLES, HORIZON_STEPS, EAST_WEST_BINS, NORTH_SOUTH_BINS), 1.0, 6.0, ((2, 4), (3, 2))),
        "variable_importance": jnp.clip(jnp.exp(jax.random.uniform(keys[2], (INPUT_VARIABLES,), jnp.float32, math.log(0.3), math.log(3.0))), 0.3, 3.0),
        "verifying_measurements": noise(keys[3], (ARCHIVE_DATES, HORIZON_STEPS, EAST_WEST_BINS, NORTH_SOUTH_BINS), 1.0, 6.0, ((0, 4), (2, 4), (3, 2))),
        "matching_dates_chosen": different_ones(keys[4], HORIZON_STEPS * EAST_WEST_BINS * NORTH_SOUTH_BINS, ARCHIVE_DATES, MATCH_NUMBER, 5120).reshape((HORIZON_STEPS, EAST_WEST_BINS, NORTH_SOUTH_BINS, MATCH_NUMBER)),
    }


def box_metric(squares):
    count_x = squares.shape[1]
    count_y = squares.shape[2]
    looped = jnp.concatenate([squares[:, count_x - 3:], squares, squares[:, :3]], axis=1)
    along = looped[:, 0:count_x]
    for shift in range(1, 7):
        along = along + looped[:, shift:shift + count_x]
    padded = jnp.pad(along, ((0, 0), (0, 0), (3, 3)))
    boxed = padded[:, :, 0:count_y]
    for shift in range(1, 7):
        boxed = boxed + padded[:, :, shift:shift + count_y]
    leads = jnp.pad(boxed, ((1, 1), (0, 0), (0, 0)))
    return (leads[:-2] + leads[1:-1] + leads[2:]) / 147.0


def reference(historical_runs, todays_outlook, variable_importance, verifying_measurements, matching_dates_chosen):
    todays_outlook_grid = todays_outlook.astype(jnp.float32)

    def one_day(fields):
        diff = fields.astype(jnp.float32) - todays_outlook_grid
        squares = jnp.sum(variable_importance[:, None, None, None] * diff * diff, axis=0)
        return box_metric(squares)

    metric = lax.map(one_day, historical_runs)
    weights = (1.0 / (metric + 1e-5)).astype(jnp.bfloat16)
    weight_last = jnp.moveaxis(weights, 0, -1)
    obs_last = jnp.moveaxis(verifying_measurements, 0, -1)
    picked_w = jnp.take_along_axis(weight_last, matching_dates_chosen, axis=-1).astype(jnp.float32)
    picked_o = jnp.take_along_axis(obs_last, matching_dates_chosen, axis=-1).astype(jnp.float32)
    numerator = jnp.sum(picked_w * picked_o, axis=-1)
    denominator = jnp.sum(picked_w, axis=-1)
    return metric, numerator / denominator
```

```python
import functools

import jax
import jax.numpy as jnp
from jax import lax
from jax.experimental import pallas as pl
from jax.experimental.pallas import tpu as pltpu
from jax.sharding import PartitionSpec as P

RIM = 3
SLOT = 8
F32 = jnp.float32
BF16 = jnp.bfloat16


def kernel(
    days, lons, runs, outlook, scale, obs, chosen, metric_out, prediction_out,
    outlook_f, lhs, band, boxed, edge, edge_in, corner, corner_in, rim, rim_in,
    bits, bits_t, packed, mask_send, mask_in, part, part_send, part_in, flip,
    near_send, near_recv, mask_ssem, mask_rsem, part_ssem, part_rsem,
):
    variables, leads, cols, own_days, rows = runs.shape
    matches = chosen.shape[1]
    share = rows // days
    groups = -(-cols // days)
    per_tile = rows // SLOT
    day, lon, lat = lax.axis_index("day"), lax.axis_index("lon"), lax.axis_index("lat")
    left, right = lax.rem(lon + lons - 1, lons), lax.rem(lon + 1, lons)
    other = 1 - lat

    nearby = [
        {"lon": left}, {"lon": right},
        {"lon": left, "lat": other}, {"lon": right, "lat": other},
        {"lat": other},
    ]
    owners = [lax.rem(day + step, days) for step in range(days)]
    barrier = pltpu.get_barrier_semaphore()
    for device in nearby + [{"day": owner} for owner in owners[1:]]:
        pl.semaphore_signal(barrier, inc=1, device_id=device, device_id_type=pl.DeviceIdType.MESH)

    lane = lax.broadcasted_iota(jnp.int32, (own_days, rows), 1)
    slot_of = lane // SLOT
    part_of = lane // share

    def send(src, dst, ssem, rsem, device):
        copy = pltpu.make_async_remote_copy(
            src_ref=src, dst_ref=dst, send_sem=ssem, recv_sem=rsem,
            device_id=device, device_id_type=pl.DeviceIdType.MESH,
        )
        copy.start()
        return copy

    for p in range(variables):
        for l in range(leads):
            outlook_f[p * leads + l] = outlook[p, l].astype(F32)

    def squares(l, x):
        total = jnp.zeros((own_days, rows), F32)
        for p in range(variables):
            diff = runs[p, l, x].astype(F32) - outlook_f[p * leads + l, pl.ds(x, 1), :]
            total = total + scale[p] * (diff * diff)
        return total.astype(BF16)

    def edge_columns(x, side):
        for l in range(leads):
            value = squares(l, x + side * (cols - RIM))
            lhs[l, x + side * (cols - RIM) + RIM, :, :rows] = value
            edge[side, l * RIM + x] = value

    for side in range(2):
        @pl.loop(0, RIM)
        def _(x):
            edge_columns(x, side)
        total = jnp.zeros((own_days, rows), F32)
        for s in range(leads * RIM):
            moved = pltpu.roll(edge[side, s].astype(F32), RIM + SLOT * s, 1)
            total = jnp.where(slot_of == s, moved, total)
        corner[side] = total.astype(BF16)

    pl.semaphore_wait(barrier, len(nearby) + days - 1)
    near = []
    for side, (device, across) in enumerate([(nearby[0], nearby[2]), (nearby[1], nearby[3])]):
        near.append(send(edge.at[side], edge_in.at[1 - side], near_send.at[side], near_recv.at[side], device))
        near.append(send(corner.at[side], corner_in.at[1 - side], near_send.at[2 + side], near_recv.at[2 + side], across))

    words = days * own_days // 32
    targets_per_word = 32 // own_days
    for t in range(bits.shape[0]):
        bits[t] = jnp.zeros((rows, rows), jnp.int32)
    for l in range(leads):
        sums = [jnp.zeros((share, cols), jnp.int32) for _ in range(words)]
        for k in range(matches):
            index = chosen[l, k]
            bit = lax.shift_left(jnp.ones_like(index), index & 31)
            word = lax.shift_right_logical(index, jnp.full_like(index, 5))
            for w in range(words):
                sums[w] = sums[w] | jnp.where(word == w, bit, 0)
        for w in range(words):
            c = w * leads + l
            at = (c % days) * share
            bits[c // days, at:at + share, :cols] = sums[w]
    for t in range(bits.shape[0]):
        bits_t[t] = bits[t].T
    group_lane = lax.broadcasted_iota(jnp.int32, (groups, rows), 1) // share
    for c in range(words * leads):
        total = jnp.zeros((groups, rows), jnp.int32)
        for i in range(days):
            moved = bits_t[c // days, pl.ds(i, groups, stride=days), :]
            shift = (share * (i - c % days)) % rows
            if shift:
                moved = pltpu.roll(moved, shift, 1)
            total = jnp.where(group_lane == i, moved, total)
        packed[c, :groups] = total

    day_row = lax.broadcasted_iota(jnp.int32, (own_days, rows), 0)

    def expand(owner, store):
        shift = day_row + lax.rem(owner, targets_per_word) * own_days
        base = (owner // targets_per_word) * leads
        for l in range(leads):
            @pl.loop(0, groups)
            def _(q):
                row = jnp.broadcast_to(packed[base + l, pl.ds(q, 1), :], (own_days, rows))
                store(l, q, (lax.shift_right_logical(row, shift) & 1).astype(F32).astype(BF16))

    masks = []
    for step in range(1, days):
        def store(l, q, value):
            mask_send[step - 1, l, q] = value
        expand(owners[step], store)
        masks.append(send(
            mask_send.at[step - 1], mask_in.at[day], mask_ssem.at[step - 1], mask_rsem.at[step - 1],
            {"day": owners[step]},
        ))

    @pl.loop(RIM, cols - RIM)
    def _(x):
        for l in range(leads):
            lhs[l, x + RIM, :, :rows] = squares(l, x)

    @pl.loop(0, leads)
    def _(l):
        for g in range(rim.shape[1]):
            total = jnp.zeros((own_days, rows), F32)
            for s in range(min(per_tile, cols - g * per_tile)):
                tile = lhs[l, g * per_tile + s + RIM, :, :rows].astype(F32)
                total = jnp.where(slot_of == s, pltpu.roll(tile, (RIM + SLOT * s) % rows, 1), total)
            rim[l, g] = total.astype(BF16)

    near.append(send(rim, rim_in, near_send.at[4], near_recv.at[4], nearby[4]))

    def own_store(l, q, value):
        mask_in[day, l, q] = value
    expand(owners[0], own_store)

    source = lax.broadcasted_iota(jnp.int32, (2 * rows, rows), 0)
    target = lax.broadcasted_iota(jnp.int32, (2 * rows, rows), 1)
    beyond = source - rows
    place = beyond - RIM + rows * other
    first = RIM * other
    inside = (source < rows) & (jnp.abs(source - target) <= RIM)
    across = (beyond >= first) & (beyond < first + RIM) & (jnp.abs(place - target) <= RIM)
    band[...] = jnp.where(inside | across, 1.0, 0.0).astype(BF16)
    part[...] = jnp.zeros(part.shape, F32)

    for copy in near:
        copy.wait()

    @pl.loop(0, leads)
    def _(l):
        for g in range(rim.shape[1]):
            tile = rim_in[l, g].astype(F32)
            for s in range(min(per_tile, cols - g * per_tile)):
                lhs[l, g * per_tile + s + RIM, :, rows:] = pltpu.roll(tile, (-SLOT * s) % rows, 1).astype(BF16)

    for side in range(2):
        tile = corner_in[side].astype(F32)
        for l in range(leads):
            for c in range(RIM):
                s = l * RIM + c
                x = side * (cols + RIM) + c
                lhs[l, x, :, :rows] = edge_in[side, s]
                lhs[l, x, :, rows:] = pltpu.roll(tile, (-SLOT * s) % rows, 1).astype(BF16)

    @pl.loop(0, leads)
    def _(l):
        flat = lhs[l].reshape((cols + 2 * RIM) * own_days, 2 * rows)
        product = jnp.dot(flat, band[...], preferred_element_type=F32)
        boxed[l] = product.reshape(cols + 2 * RIM, own_days, rows)

    for copy in masks:
        copy.wait()

    def chunk(q, count):
        start = q * days
        window = []
        for l in range(leads):
            y = [boxed[l, start + i] for i in range(count + 2 * RIM)]
            two = [y[i] + y[i + 1] for i in range(count + 5)]
            window.append([two[i] + two[i + 2] + (two[i + 4] + y[i + 6]) for i in range(count)])
        for l in range(leads):
            masked = [mask_in[g, l, q].astype(F32) for g in range(days)]
            for i in range(count):
                total = window[l][i]
                if l > 0:
                    total = total + window[l - 1][i]
                if l < leads - 1:
                    total = total + window[l + 1][i]
                metric = total * (1.0 / 147.0)
                metric_out[l, start + i] = metric
                weight = (1.0 / (metric + 1e-5)).astype(BF16).astype(F32)
                picked = jnp.zeros((own_days, rows), F32)
                for g in range(days):
                    shift = (share * (g - i)) % rows
                    moved = pltpu.roll(masked[g], shift, 1) if shift else masked[g]
                    picked = jnp.where(part_of == g, moved, picked)
                weight = weight * picked
                part[l, pl.ds(start + i, 1), :] = jnp.sum(
                    weight * obs[l, start + i].astype(F32), axis=0, keepdims=True)
                part[leads + l, pl.ds(start + i, 1), :] = jnp.sum(weight, axis=0, keepdims=True)

    @pl.loop(0, cols // days)
    def _(q):
        chunk(q, days)
    if cols % days:
        chunk(cols // days, cols % days)

    wide = part.shape[1]
    wide_part = lax.broadcasted_iota(jnp.int32, (wide, rows), 1) // share
    partials = []
    for step in [*range(1, days), 0]:
        owner = owners[step]
        for t in range(2):
            total = jnp.ones((wide, rows), F32)
            for l in range(leads):
                shift = lax.rem(share * (l - owner) + rows * days, rows)
                total = jnp.where(wide_part == l, pltpu.roll(part[t * leads + l], shift, 1), total)
            if step:
                part_send[step - 1, t] = total
            else:
                part_in[0, t] = total
        if step:
            partials.append(send(
                part_send.at[step - 1], part_in.at[step], part_ssem.at[step - 1], part_rsem.at[step - 1],
                {"day": owner},
            ))
    flip[...] = jnp.zeros(flip.shape, F32)
    for copy in partials:
        copy.wait()
    numerator, denominator = part_in[0, 0], part_in[0, 1]
    for step in range(1, days):
        numerator = numerator + part_in[step, 0]
        denominator = denominator + part_in[step, 1]
    flip[:wide] = numerator / denominator
    turned = flip[...].T
    for l in range(leads):
        prediction_out[l] = turned[l * share:(l + 1) * share, :cols]


def on_device(days, lons, runs, outlook, scale, obs, chosen):
    runs = jnp.transpose(runs, (1, 2, 3, 0, 4))
    obs = jnp.transpose(obs, (1, 2, 0, 3))
    chosen = jnp.transpose(chosen, (0, 3, 2, 1))
    variables, leads, cols, own_days, rows = runs.shape
    share = rows // days
    groups = -(-cols // days)
    words = days * own_days // 32
    tiles = -(-words * leads // days)
    rims = -(-cols // (rows // SLOT))
    wide = -(-cols // 8) * 8
    tile = (own_days, rows)
    vmem = pl.BlockSpec(memory_space=pltpu.VMEM)
    metric, prediction = pl.pallas_call(
        functools.partial(kernel, days, lons),
        out_shape=(
            jax.ShapeDtypeStruct((leads, cols) + tile, F32),
            jax.ShapeDtypeStruct((leads, share, cols), F32),
        ),
        in_specs=[vmem, vmem, pl.BlockSpec(memory_space=pltpu.SMEM), vmem, vmem],
        out_specs=(vmem, vmem),
        scratch_shapes=[
            pltpu.VMEM((variables * leads, cols, rows), F32),
            pltpu.VMEM((leads, cols + 2 * RIM, own_days, 2 * rows), BF16),
            pltpu.VMEM((2 * rows, rows), BF16),
            pltpu.VMEM((leads, cols + 2 * RIM) + tile, F32),
            pltpu.VMEM((2, leads * RIM) + tile, BF16),
            pltpu.VMEM((2, leads * RIM) + tile, BF16),
            pltpu.VMEM((2,) + tile, BF16),
            pltpu.VMEM((2,) + tile, BF16),
            pltpu.VMEM((leads, rims) + tile, BF16),
            pltpu.VMEM((leads, rims) + tile, BF16),
            pltpu.VMEM((tiles, rows, rows), jnp.int32),
            pltpu.VMEM((tiles, rows, rows), jnp.int32),
            pltpu.VMEM((words * leads, -(-groups // 8) * 8, rows), jnp.int32),
            pltpu.VMEM((days - 1, leads, groups) + tile, BF16),
            pltpu.VMEM((days, leads, groups) + tile, BF16),
            pltpu.VMEM((2 * leads, wide, rows), F32),
            pltpu.VMEM((days - 1, 2, wide, rows), F32),
            pltpu.VMEM((days, 2, wide, rows), F32),
            pltpu.VMEM((rows, rows), F32),
            pltpu.SemaphoreType.DMA((5,)),
            pltpu.SemaphoreType.DMA((5,)),
            pltpu.SemaphoreType.DMA((days - 1,)),
            pltpu.SemaphoreType.DMA((days - 1,)),
            pltpu.SemaphoreType.DMA((days - 1,)),
            pltpu.SemaphoreType.DMA((days - 1,)),
        ],
        compiler_params=pltpu.CompilerParams(
            collective_id=0, has_side_effects=True, vmem_limit_bytes=48 * 2**20
        ),
    )(runs, outlook, scale, obs, chosen)
    return jnp.transpose(metric, (2, 0, 1, 3)), jnp.transpose(prediction, (0, 2, 1))


def solution(mesh):
    in_specs = (
        P("day", None, None, "lon", "lat"),
        P(None, None, "lon", "lat"),
        P(),
        P("day", None, "lon", "lat"),
        P(None, "lon", ("lat", "day"), None),
    )
    out_specs = (P("day", None, "lon", "lat"), P(None, "lon", ("lat", "day")))
    return jax.shard_map(
        functools.partial(on_device, mesh.shape["day"], mesh.shape["lon"]),
        mesh=mesh, in_specs=in_specs, out_specs=out_specs, check_vma=False,
    )
```

```python
import functools

import jax
import jax.numpy as jnp
from jax import lax
from jax.experimental import pallas as pl
from jax.experimental.pallas import tpu as pltpu
from jax.sharding import PartitionSpec as P

RIM = 3
SLOT = 8
F32 = jnp.float32
BF16 = jnp.bfloat16


def kernel(
    days, lons, runs_hbm, outlook_hbm, scale, obs_hbm, chosen_hbm, metric_out, prediction_out,
    runs, outlook, obs, chosen, load_sem,
    outlook_f, lhs, band, boxed, edge, edge_in, corner, corner_in, rim, rim_in,
    bits, bits_t, packed, mask_send, mask_in, part, part_send, part_in, flip,
    near_send, near_recv, mask_ssem, mask_rsem, part_ssem, part_rsem,
):
    variables, leads, cols, own_days, rows = runs.shape
    matches = chosen.shape[1]
    share = rows // days
    groups = -(-cols // days)
    per_tile = rows // SLOT
    day, lon, lat = lax.axis_index("day"), lax.axis_index("lon"), lax.axis_index("lat")
    left, right = lax.rem(lon + lons - 1, lons), lax.rem(lon + 1, lons)
    other = 1 - lat

    nearby = [
        {"lon": left}, {"lon": right},
        {"lon": left, "lat": other}, {"lon": right, "lat": other},
        {"lat": other},
    ]
    owners = [lax.rem(day + step, days) for step in range(days)]
    loads = [
        pltpu.make_async_copy(outlook_hbm, outlook, load_sem.at[0]),
        pltpu.make_async_copy(runs_hbm.at[:, :, :RIM], runs.at[:, :, :RIM], load_sem.at[1]),
        pltpu.make_async_copy(runs_hbm.at[:, :, cols - RIM:], runs.at[:, :, cols - RIM:], load_sem.at[2]),
        pltpu.make_async_copy(chosen_hbm, chosen, load_sem.at[3]),
        pltpu.make_async_copy(
            runs_hbm.at[:, :, RIM:cols - RIM], runs.at[:, :, RIM:cols - RIM], load_sem.at[4]),
        pltpu.make_async_copy(obs_hbm, obs, load_sem.at[5]),
    ]
    for load in loads:
        load.start()

    barrier = pltpu.get_barrier_semaphore()
    for device in nearby + [{"day": owner} for owner in owners[1:]]:
        pl.semaphore_signal(barrier, inc=1, device_id=device, device_id_type=pl.DeviceIdType.MESH)

    lane = lax.broadcasted_iota(jnp.int32, (own_days, rows), 1)
    slot_of = lane // SLOT
    part_of = lane // share

    def send(src, dst, ssem, rsem, device):
        copy = pltpu.make_async_remote_copy(
            src_ref=src, dst_ref=dst, send_sem=ssem, recv_sem=rsem,
            device_id=device, device_id_type=pl.DeviceIdType.MESH,
        )
        copy.start()
        return copy

    loads[0].wait()
    for p in range(variables):
        for l in range(leads):
            outlook_f[p * leads + l] = outlook[p, l].astype(F32)

    def squares(l, x):
        total = jnp.zeros((own_days, rows), F32)
        for p in range(variables):
            diff = runs[p, l, x].astype(F32) - outlook_f[p * leads + l, pl.ds(x, 1), :]
            total = total + scale[p] * (diff * diff)
        return total.astype(BF16)

    def edge_columns(x, side):
        for l in range(leads):
            value = squares(l, x + side * (cols - RIM))
            lhs[l, x + side * (cols - RIM) + RIM, :, :rows] = value
            edge[side, l * RIM + x] = value

    for side in range(2):
        loads[1 + side].wait()

        @pl.loop(0, RIM)
        def _(x):
            edge_columns(x, side)
        total = jnp.zeros((own_days, rows), F32)
        for s in range(leads * RIM):
            moved = pltpu.roll(edge[side, s].astype(F32), RIM + SLOT * s, 1)
            total = jnp.where(slot_of == s, moved, total)
        corner[side] = total.astype(BF16)

    pl.semaphore_wait(barrier, len(nearby) + days - 1)
    near = []
    for side, (device, across) in enumerate([(nearby[0], nearby[2]), (nearby[1], nearby[3])]):
        near.append(send(edge.at[side], edge_in.at[1 - side], near_send.at[side], near_recv.at[side], device))
        near.append(send(corner.at[side], corner_in.at[1 - side], near_send.at[2 + side], near_recv.at[2 + side], across))

    loads[3].wait()
    words = days * own_days // 32
    targets_per_word = 32 // own_days
    for t in range(bits.shape[0]):
        bits[t] = jnp.zeros((rows, rows), jnp.int32)
    for l in range(leads):
        sums = [jnp.zeros((share, cols), jnp.int32) for _ in range(words)]
        for k in range(matches):
            index = chosen[l, k]
            bit = lax.shift_left(jnp.ones_like(index), index & 31)
            word = lax.shift_right_logical(index, jnp.full_like(index, 5))
            for w in range(words):
                sums[w] = sums[w] | jnp.where(word == w, bit, 0)
        for w in range(words):
            c = w * leads + l
            at = (c % days) * share
            bits[c // days, at:at + share, :cols] = sums[w]
    for t in range(bits.shape[0]):
        bits_t[t] = bits[t].T
    group_lane = lax.broadcasted_iota(jnp.int32, (groups, rows), 1) // share
    for c in range(words * leads):
        total = jnp.zeros((groups, rows), jnp.int32)
        for i in range(days):
            moved = bits_t[c // days, pl.ds(i, groups, stride=days), :]
            shift = (share * (i - c % days)) % rows
            if shift:
                moved = pltpu.roll(moved, shift, 1)
            total = jnp.where(group_lane == i, moved, total)
        packed[c, :groups] = total

    day_row = lax.broadcasted_iota(jnp.int32, (own_days, rows), 0)

    def expand(owner, store):
        shift = day_row + lax.rem(owner, targets_per_word) * own_days
        base = (owner // targets_per_word) * leads
        for l in range(leads):
            @pl.loop(0, groups)
            def _(q):
                row = jnp.broadcast_to(packed[base + l, pl.ds(q, 1), :], (own_days, rows))
                store(l, q, (lax.shift_right_logical(row, shift) & 1).astype(F32).astype(BF16))

    masks = []
    for step in range(1, days):
        def store(l, q, value):
            mask_send[step - 1, l, q] = value
        expand(owners[step], store)
        masks.append(send(
            mask_send.at[step - 1], mask_in.at[day], mask_ssem.at[step - 1], mask_rsem.at[step - 1],
            {"day": owners[step]},
        ))

    loads[4].wait()

    @pl.loop(RIM, cols - RIM)
    def _(x):
        for l in range(leads):
            lhs[l, x + RIM, :, :rows] = squares(l, x)

    @pl.loop(0, leads)
    def _(l):
        for g in range(rim.shape[1]):
            total = jnp.zeros((own_days, rows), F32)
            for s in range(min(per_tile, cols - g * per_tile)):
                tile = lhs[l, g * per_tile + s + RIM, :, :rows].astype(F32)
                total = jnp.where(slot_of == s, pltpu.roll(tile, (RIM + SLOT * s) % rows, 1), total)
            rim[l, g] = total.astype(BF16)

    near.append(send(rim, rim_in, near_send.at[4], near_recv.at[4], nearby[4]))

    def own_store(l, q, value):
        mask_in[day, l, q] = value
    expand(owners[0], own_store)

    source = lax.broadcasted_iota(jnp.int32, (2 * rows, rows), 0)
    target = lax.broadcasted_iota(jnp.int32, (2 * rows, rows), 1)
    beyond = source - rows
    place = beyond - RIM + rows * other
    first = RIM * other
    inside = (source < rows) & (jnp.abs(source - target) <= RIM)
    across = (beyond >= first) & (beyond < first + RIM) & (jnp.abs(place - target) <= RIM)
    band[...] = jnp.where(inside | across, 1.0, 0.0).astype(BF16)
    part[...] = jnp.zeros(part.shape, F32)

    for copy in near:
        copy.wait()

    @pl.loop(0, leads)
    def _(l):
        for g in range(rim.shape[1]):
            tile = rim_in[l, g].astype(F32)
            for s in range(min(per_tile, cols - g * per_tile)):
                lhs[l, g * per_tile + s + RIM, :, rows:] = pltpu.roll(tile, (-SLOT * s) % rows, 1).astype(BF16)

    for side in range(2):
        tile = corner_in[side].astype(F32)
        for l in range(leads):
            for c in range(RIM):
                s = l * RIM + c
                x = side * (cols + RIM) + c
                lhs[l, x, :, :rows] = edge_in[side, s]
                lhs[l, x, :, rows:] = pltpu.roll(tile, (-SLOT * s) % rows, 1).astype(BF16)

    @pl.loop(0, leads)
    def _(l):
        flat = lhs[l].reshape((cols + 2 * RIM) * own_days, 2 * rows)
        product = jnp.dot(flat, band[...], preferred_element_type=F32)
        boxed[l] = product.reshape(cols + 2 * RIM, own_days, rows)

    loads[5].wait()
    for copy in masks:
        copy.wait()

    def chunk(q, count):
        start = q * days
        window = []
        for l in range(leads):
            y = [boxed[l, start + i] for i in range(count + 2 * RIM)]
            two = [y[i] + y[i + 1] for i in range(count + 5)]
            window.append([two[i] + two[i + 2] + (two[i + 4] + y[i + 6]) for i in range(count)])
        for l in range(leads):
            masked = [mask_in[g, l, q].astype(F32) for g in range(days)]
            for i in range(count):
                total = window[l][i]
                if l > 0:
                    total = total + window[l - 1][i]
                if l < leads - 1:
                    total = total + window[l + 1][i]
                metric = total * (1.0 / 147.0)
                metric_out[l, start + i] = metric
                weight = (1.0 / (metric + 1e-5)).astype(BF16).astype(F32)
                picked = jnp.zeros((own_days, rows), F32)
                for g in range(days):
                    shift = (share * (g - i)) % rows
                    moved = pltpu.roll(masked[g], shift, 1) if shift else masked[g]
                    picked = jnp.where(part_of == g, moved, picked)
                weight = weight * picked
                part[l, pl.ds(start + i, 1), :] = jnp.sum(
                    weight * obs[l, start + i].astype(F32), axis=0, keepdims=True)
                part[leads + l, pl.ds(start + i, 1), :] = jnp.sum(weight, axis=0, keepdims=True)

    @pl.loop(0, cols // days)
    def _(q):
        chunk(q, days)
    if cols % days:
        chunk(cols // days, cols % days)

    wide = part.shape[1]
    wide_part = lax.broadcasted_iota(jnp.int32, (wide, rows), 1) // share
    partials = []
    for step in [*range(1, days), 0]:
        owner = owners[step]
        for t in range(2):
            total = jnp.ones((wide, rows), F32)
            for l in range(leads):
                shift = lax.rem(share * (l - owner) + rows * days, rows)
                total = jnp.where(wide_part == l, pltpu.roll(part[t * leads + l], shift, 1), total)
            if step:
                part_send[step - 1, t] = total
            else:
                part_in[0, t] = total
        if step:
            partials.append(send(
                part_send.at[step - 1], part_in.at[step], part_ssem.at[step - 1], part_rsem.at[step - 1],
                {"day": owner},
            ))
    flip[...] = jnp.zeros(flip.shape, F32)
    for copy in partials:
        copy.wait()
    numerator, denominator = part_in[0, 0], part_in[0, 1]
    for step in range(1, days):
        numerator = numerator + part_in[step, 0]
        denominator = denominator + part_in[step, 1]
    flip[:wide] = numerator / denominator
    turned = flip[...].T
    for l in range(leads):
        prediction_out[l] = turned[l * share:(l + 1) * share, :cols]


def on_device(days, lons, runs, outlook, scale, obs, chosen):
    runs = jnp.transpose(runs, (1, 2, 3, 0, 4))
    obs = jnp.transpose(obs, (1, 2, 0, 3))
    chosen = jnp.transpose(chosen, (0, 3, 2, 1))
    variables, leads, cols, own_days, rows = runs.shape
    share = rows // days
    groups = -(-cols // days)
    words = days * own_days // 32
    tiles = -(-words * leads // days)
    rims = -(-cols // (rows // SLOT))
    wide = -(-cols // 8) * 8
    tile = (own_days, rows)
    vmem = pl.BlockSpec(memory_space=pltpu.VMEM)
    hbm = pl.BlockSpec(memory_space=pltpu.HBM)
    metric, prediction = pl.pallas_call(
        functools.partial(kernel, days, lons),
        out_shape=(
            jax.ShapeDtypeStruct((leads, cols) + tile, F32),
            jax.ShapeDtypeStruct((leads, share, cols), F32),
        ),
        in_specs=[hbm, hbm, pl.BlockSpec(memory_space=pltpu.SMEM), hbm, hbm],
        out_specs=(vmem, vmem),
        scratch_shapes=[
            pltpu.VMEM(runs.shape, BF16),
            pltpu.VMEM(outlook.shape, BF16),
            pltpu.VMEM(obs.shape, BF16),
            pltpu.VMEM(chosen.shape, jnp.int32),
            pltpu.SemaphoreType.DMA((6,)),
            pltpu.VMEM((variables * leads, cols, rows), F32),
            pltpu.VMEM((leads, cols + 2 * RIM, own_days, 2 * rows), BF16),
            pltpu.VMEM((2 * rows, rows), BF16),
            pltpu.VMEM((leads, cols + 2 * RIM) + tile, F32),
            pltpu.VMEM((2, leads * RIM) + tile, BF16),
            pltpu.VMEM((2, leads * RIM) + tile, BF16),
            pltpu.VMEM((2,) + tile, BF16),
            pltpu.VMEM((2,) + tile, BF16),
            pltpu.VMEM((leads, rims) + tile, BF16),
            pltpu.VMEM((leads, rims) + tile, BF16),
            pltpu.VMEM((tiles, rows, rows), jnp.int32),
            pltpu.VMEM((tiles, rows, rows), jnp.int32),
            pltpu.VMEM((words * leads, -(-groups // 8) * 8, rows), jnp.int32),
            pltpu.VMEM((days - 1, leads, groups) + tile, BF16),
            pltpu.VMEM((days, leads, groups) + tile, BF16),
            pltpu.VMEM((2 * leads, wide, rows), F32),
            pltpu.VMEM((days - 1, 2, wide, rows), F32),
            pltpu.VMEM((days, 2, wide, rows), F32),
            pltpu.VMEM((rows, rows), F32),
            pltpu.SemaphoreType.DMA((5,)),
            pltpu.SemaphoreType.DMA((5,)),
            pltpu.SemaphoreType.DMA((days - 1,)),
            pltpu.SemaphoreType.DMA((days - 1,)),
            pltpu.SemaphoreType.DMA((days - 1,)),
            pltpu.SemaphoreType.DMA((days - 1,)),
        ],
        compiler_params=pltpu.CompilerParams(
            collective_id=0, has_side_effects=True, vmem_limit_bytes=48 * 2**20
        ),
    )(runs, outlook, scale, obs, chosen)
    return jnp.transpose(metric, (2, 0, 1, 3)), jnp.transpose(prediction, (0, 2, 1))


def solution(mesh):
    in_specs = (
        P("day", None, None, "lon", "lat"),
        P(None, None, "lon", "lat"),
        P(),
        P("day", None, "lon", "lat"),
        P(None, "lon", ("lat", "day"), None),
    )
    out_specs = (P("day", None, "lon", "lat"), P(None, "lon", ("lat", "day")))
    return jax.shard_map(
        functools.partial(on_device, mesh.shape["day"], mesh.shape["lon"]),
        mesh=mesh, in_specs=in_specs, out_specs=out_specs, check_vma=False,
    )
```

```python
import functools

import jax
import jax.numpy as jnp
from jax import lax
from jax.experimental import pallas as pl
from jax.experimental.pallas import tpu as pltpu
from jax.sharding import PartitionSpec as P

RIM = 3
SLOT = 8
F32 = jnp.float32
BF16 = jnp.bfloat16


def kernel(
    days, lons, runs_hbm, outlook_hbm, scale, obs_hbm, chosen_hbm, metric_out, prediction_out,
    runs, outlook, obs, chosen, metric_v, weights, load_sem,
    outlook_f, lhs, band, boxed, edge, edge_in, corner, corner_in, rim, rim_in,
    bits, bits_t, packed, mask_send, mask_in, part, part_send, part_in, flip,
    near_send, near_recv, mask_ssem, mask_rsem, part_ssem, part_rsem,
):
    variables, leads, cols, own_days, rows = runs.shape
    matches = chosen.shape[1]
    share = rows // days
    groups = -(-cols // days)
    per_tile = rows // SLOT
    day, lon, lat = lax.axis_index("day"), lax.axis_index("lon"), lax.axis_index("lat")
    left, right = lax.rem(lon + lons - 1, lons), lax.rem(lon + 1, lons)
    other = 1 - lat

    nearby = [
        {"lon": left}, {"lon": right},
        {"lon": left, "lat": other}, {"lon": right, "lat": other},
        {"lat": other},
    ]
    owners = [lax.rem(day + step, days) for step in range(days)]
    loads = [
        pltpu.make_async_copy(chosen_hbm, chosen, load_sem.at[3]),
        pltpu.make_async_copy(outlook_hbm, outlook, load_sem.at[0]),
        pltpu.make_async_copy(runs_hbm.at[:, :, :RIM], runs.at[:, :, :RIM], load_sem.at[1]),
        pltpu.make_async_copy(runs_hbm.at[:, :, cols - RIM:], runs.at[:, :, cols - RIM:], load_sem.at[2]),
        pltpu.make_async_copy(
            runs_hbm.at[:, :, RIM:cols - RIM], runs.at[:, :, RIM:cols - RIM], load_sem.at[4]),
        pltpu.make_async_copy(obs_hbm, obs, load_sem.at[5]),
    ]
    for load in loads:
        load.start()

    barrier = pltpu.get_barrier_semaphore()
    for device in nearby + [{"day": owner} for owner in owners[1:]]:
        pl.semaphore_signal(barrier, inc=1, device_id=device, device_id_type=pl.DeviceIdType.MESH)

    lane = lax.broadcasted_iota(jnp.int32, (own_days, rows), 1)
    slot_of = lane // SLOT
    part_of = lane // share

    def send(src, dst, ssem, rsem, device):
        copy = pltpu.make_async_remote_copy(
            src_ref=src, dst_ref=dst, send_sem=ssem, recv_sem=rsem,
            device_id=device, device_id_type=pl.DeviceIdType.MESH,
        )
        copy.start()
        return copy

    loads[0].wait()
    words = days * own_days // 32
    targets_per_word = 32 // own_days
    for t in range(bits.shape[0]):
        bits[t] = jnp.zeros((rows, rows), jnp.int32)
    for l in range(leads):
        sums = [jnp.zeros((share, cols), jnp.int32) for _ in range(words)]
        for k in range(matches):
            index = chosen[l, k]
            bit = lax.shift_left(jnp.ones_like(index), index & 31)
            word = lax.shift_right_logical(index, jnp.full_like(index, 5))
            for w in range(words):
                sums[w] = sums[w] | jnp.where(word == w, bit, 0)
        for w in range(words):
            c = w * leads + l
            at = (c % days) * share
            bits[c // days, at:at + share, :cols] = sums[w]
    for t in range(bits.shape[0]):
        bits_t[t] = bits[t].T
    group_lane = lax.broadcasted_iota(jnp.int32, (groups, rows), 1) // share
    for c in range(words * leads):
        total = jnp.zeros((groups, rows), jnp.int32)
        for i in range(days):
            moved = bits_t[c // days, pl.ds(i, groups, stride=days), :]
            shift = (share * (i - c % days)) % rows
            if shift:
                moved = pltpu.roll(moved, shift, 1)
            total = jnp.where(group_lane == i, moved, total)
        packed[c, :groups] = total

    day_row = lax.broadcasted_iota(jnp.int32, (own_days, rows), 0)

    def expand(owner, l, store):
        shift = day_row + lax.rem(owner, targets_per_word) * own_days
        base = (owner // targets_per_word) * leads

        @pl.loop(0, groups)
        def _(q):
            row = jnp.broadcast_to(packed[base + l, pl.ds(q, 1), :], (own_days, rows))
            store(q, (lax.shift_right_logical(row, shift) & 1).astype(F32).astype(BF16))

    masks = [[] for _ in range(leads)]

    def send_masks(l):
        for step in range(1, days):
            def store(q, value):
                mask_send[step - 1, l, q] = value
            expand(owners[step], l, store)
            masks[l].append(send(
                mask_send.at[step - 1, l], mask_in.at[day, l],
                mask_ssem.at[step - 1, l], mask_rsem.at[step - 1, l], {"day": owners[step]},
            ))

    pl.semaphore_wait(barrier, len(nearby) + days - 1)
    send_masks(0)
    loads[1].wait()
    for p in range(variables):
        for l in range(leads):
            outlook_f[p * leads + l] = outlook[p, l].astype(F32)

    def squares(l, x):
        total = jnp.zeros((own_days, rows), F32)
        for p in range(variables):
            diff = runs[p, l, x].astype(F32) - outlook_f[p * leads + l, pl.ds(x, 1), :]
            total = total + scale[p] * (diff * diff)
        return total.astype(BF16)

    def edge_columns(x, side):
        for l in range(leads):
            value = squares(l, x + side * (cols - RIM))
            lhs[l, x + side * (cols - RIM) + RIM, :, :rows] = value
            edge[side, l * RIM + x] = value

    for side in range(2):
        loads[2 + side].wait()

        @pl.loop(0, RIM)
        def _(x):
            edge_columns(x, side)
        total = jnp.zeros((own_days, rows), F32)
        for s in range(leads * RIM):
            moved = pltpu.roll(edge[side, s].astype(F32), RIM + SLOT * s, 1)
            total = jnp.where(slot_of == s, moved, total)
        corner[side] = total.astype(BF16)

    near = []
    for side, (device, across) in enumerate([(nearby[0], nearby[2]), (nearby[1], nearby[3])]):
        near.append(send(edge.at[side], edge_in.at[1 - side], near_send.at[side], near_recv.at[side], device))
        near.append(send(corner.at[side], corner_in.at[1 - side], near_send.at[2 + side], near_recv.at[2 + side], across))

    for l in range(1, leads):
        send_masks(l)

    loads[4].wait()

    @pl.loop(RIM, cols - RIM)
    def _(x):
        for l in range(leads):
            lhs[l, x + RIM, :, :rows] = squares(l, x)

    @pl.loop(0, leads)
    def _(l):
        for g in range(rim.shape[1]):
            total = jnp.zeros((own_days, rows), F32)
            for s in range(min(per_tile, cols - g * per_tile)):
                tile = lhs[l, g * per_tile + s + RIM, :, :rows].astype(F32)
                total = jnp.where(slot_of == s, pltpu.roll(tile, (RIM + SLOT * s) % rows, 1), total)
            rim[l, g] = total.astype(BF16)

    near.append(send(rim, rim_in, near_send.at[4], near_recv.at[4], nearby[4]))

    for l in range(leads):
        def own_store(q, value):
            mask_in[day, l, q] = value
        expand(owners[0], l, own_store)

    source = lax.broadcasted_iota(jnp.int32, (2 * rows, rows), 0)
    target = lax.broadcasted_iota(jnp.int32, (2 * rows, rows), 1)
    beyond = source - rows
    place = beyond - RIM + rows * other
    first = RIM * other
    inside = (source < rows) & (jnp.abs(source - target) <= RIM)
    across = (beyond >= first) & (beyond < first + RIM) & (jnp.abs(place - target) <= RIM)
    band[...] = jnp.where(inside | across, 1.0, 0.0).astype(BF16)
    part[...] = jnp.zeros(part.shape, F32)

    for copy in near:
        copy.wait()

    @pl.loop(0, leads)
    def _(l):
        for g in range(rim.shape[1]):
            tile = rim_in[l, g].astype(F32)
            for s in range(min(per_tile, cols - g * per_tile)):
                lhs[l, g * per_tile + s + RIM, :, rows:] = pltpu.roll(tile, (-SLOT * s) % rows, 1).astype(BF16)

    for side in range(2):
        tile = corner_in[side].astype(F32)
        for l in range(leads):
            for c in range(RIM):
                s = l * RIM + c
                x = side * (cols + RIM) + c
                lhs[l, x, :, :rows] = edge_in[side, s]
                lhs[l, x, :, rows:] = pltpu.roll(tile, (-SLOT * s) % rows, 1).astype(BF16)

    @pl.loop(0, leads)
    def _(l):
        flat = lhs[l].reshape((cols + 2 * RIM) * own_days, 2 * rows)
        product = jnp.dot(flat, band[...], preferred_element_type=F32)
        boxed[l] = product.reshape(cols + 2 * RIM, own_days, rows)

    def weigh(start, count):
        window = []
        for l in range(leads):
            y = [boxed[l, start + i] for i in range(count + 2 * RIM)]
            two = [y[i] + y[i + 1] for i in range(count + 5)]
            window.append([two[i] + two[i + 2] + (two[i + 4] + y[i + 6]) for i in range(count)])
        for l in range(leads):
            for i in range(count):
                total = window[l][i]
                if l > 0:
                    total = total + window[l - 1][i]
                if l < leads - 1:
                    total = total + window[l + 1][i]
                metric = total * (1.0 / 147.0)
                metric_v[l, start + i] = metric
                weights[l, start + i] = (1.0 / (metric + 1e-5)).astype(BF16)

    @pl.loop(0, cols // days)
    def _(q):
        weigh(q * days, days)
    if cols % days:
        weigh(cols - cols % days, cols % days)
    metric_copy = pltpu.make_async_copy(metric_v, metric_out, load_sem.at[6])
    metric_copy.start()

    loads[5].wait()

    def pick(l, q, count):
        masked = [mask_in[g, l, q].astype(F32) for g in range(days)]
        for i in range(count):
            x = q * days + i
            picked = jnp.zeros((own_days, rows), F32)
            for g in range(days):
                shift = (share * (g - i)) % rows
                moved = pltpu.roll(masked[g], shift, 1) if shift else masked[g]
                picked = jnp.where(part_of == g, moved, picked)
            weight = weights[l, x].astype(F32) * picked
            part[0, pl.ds(x, 1), :] = jnp.sum(weight * obs[l, x].astype(F32), axis=0, keepdims=True)
            part[1, pl.ds(x, 1), :] = jnp.sum(weight, axis=0, keepdims=True)

    half = part.shape[1] // 2
    half_part = lax.broadcasted_iota(jnp.int32, (half, rows), 1) // share
    partials = []
    for l in range(leads):
        for copy in masks[l]:
            copy.wait()

        @pl.loop(0, cols // days)
        def _(q):
            pick(l, q, days)
        if cols % days:
            pick(l, cols // days, cols % days)

        for step in [*range(1, days), 0]:
            total = jnp.zeros((half, rows), F32)
            for slot in range(4):
                shift = lax.rem(share * (slot - owners[step]) + rows * days, rows)
                at = half * (slot // 2)
                moved = pltpu.roll(part[slot % 2, at:at + half, :], shift, 1)
                total = jnp.where(half_part == slot, moved, total)
            if step:
                part_send[step - 1, l] = total
                partials.append(send(
                    part_send.at[step - 1, l], part_in.at[step, l],
                    part_ssem.at[step - 1, l], part_rsem.at[step - 1, l], {"day": owners[step]},
                ))
            else:
                part_in[0, l] = total
    flip[...] = jnp.zeros(flip.shape, F32)
    metric_copy.wait()
    for copy in partials:
        copy.wait()
    halves = [jnp.zeros((half, rows), F32) for _ in range(2)]
    for l in range(leads):
        total = part_in[0, l]
        for step in range(1, days):
            total = total + part_in[step, l]
        ratio = total / pltpu.roll(total, rows - share, 1)
        for h in range(2):
            shift = (share * (l - 2 * h)) % rows
            moved = pltpu.roll(ratio, shift, 1) if shift else ratio
            halves[h] = jnp.where(half_part == l, moved, halves[h])
    for h in range(2):
        flip[half * h:half * (h + 1)] = halves[h]
    turned = flip[...].T
    for l in range(leads):
        prediction_out[l] = turned[l * share:(l + 1) * share, :cols]


def on_device(days, lons, runs, outlook, scale, obs, chosen):
    runs = jnp.transpose(runs, (1, 2, 3, 0, 4))
    obs = jnp.transpose(obs, (1, 2, 0, 3))
    chosen = jnp.transpose(chosen, (0, 3, 2, 1))
    variables, leads, cols, own_days, rows = runs.shape
    share = rows // days
    groups = -(-cols // days)
    words = days * own_days // 32
    tiles = -(-words * leads // days)
    rims = -(-cols // (rows // SLOT))
    wide = -(-cols // 16) * 16
    tile = (own_days, rows)
    vmem = pl.BlockSpec(memory_space=pltpu.VMEM)
    hbm = pl.BlockSpec(memory_space=pltpu.HBM)
    metric, prediction = pl.pallas_call(
        functools.partial(kernel, days, lons),
        out_shape=(
            jax.ShapeDtypeStruct((leads, cols) + tile, F32),
            jax.ShapeDtypeStruct((leads, share, cols), F32),
        ),
        in_specs=[hbm, hbm, pl.BlockSpec(memory_space=pltpu.SMEM), hbm, hbm],
        out_specs=(hbm, vmem),
        scratch_shapes=[
            pltpu.VMEM(runs.shape, BF16),
            pltpu.VMEM(outlook.shape, BF16),
            pltpu.VMEM(obs.shape, BF16),
            pltpu.VMEM(chosen.shape, jnp.int32),
            pltpu.VMEM((leads, cols) + tile, F32),
            pltpu.VMEM((leads, cols) + tile, BF16),
            pltpu.SemaphoreType.DMA((7,)),
            pltpu.VMEM((variables * leads, cols, rows), F32),
            pltpu.VMEM((leads, cols + 2 * RIM, own_days, 2 * rows), BF16),
            pltpu.VMEM((2 * rows, rows), BF16),
            pltpu.VMEM((leads, cols + 2 * RIM) + tile, F32),
            pltpu.VMEM((2, leads * RIM) + tile, BF16),
            pltpu.VMEM((2, leads * RIM) + tile, BF16),
            pltpu.VMEM((2,) + tile, BF16),
            pltpu.VMEM((2,) + tile, BF16),
            pltpu.VMEM((leads, rims) + tile, BF16),
            pltpu.VMEM((leads, rims) + tile, BF16),
            pltpu.VMEM((tiles, rows, rows), jnp.int32),
            pltpu.VMEM((tiles, rows, rows), jnp.int32),
            pltpu.VMEM((words * leads, -(-groups // 8) * 8, rows), jnp.int32),
            pltpu.VMEM((days - 1, leads, groups) + tile, BF16),
            pltpu.VMEM((days, leads, groups) + tile, BF16),
            pltpu.VMEM((2, wide, rows), F32),
            pltpu.VMEM((days - 1, leads, wide // 2, rows), F32),
            pltpu.VMEM((days, leads, wide // 2, rows), F32),
            pltpu.VMEM((rows, rows), F32),
            pltpu.SemaphoreType.DMA((5,)),
            pltpu.SemaphoreType.DMA((5,)),
            pltpu.SemaphoreType.DMA((days - 1, leads)),
            pltpu.SemaphoreType.DMA((days - 1, leads)),
            pltpu.SemaphoreType.DMA((days - 1, leads)),
            pltpu.SemaphoreType.DMA((days - 1, leads)),
        ],
        compiler_params=pltpu.CompilerParams(
            collective_id=0, has_side_effects=True, vmem_limit_bytes=64 * 2**20 - 2**16
        ),
    )(runs, outlook, scale, obs, chosen)
    return jnp.transpose(metric, (2, 0, 1, 3)), jnp.transpose(prediction, (0, 2, 1))


def solution(mesh):
    in_specs = (
        P("day", None, None, "lon", "lat"),
        P(None, None, "lon", "lat"),
        P(),
        P("day", None, "lon", "lat"),
        P(None, "lon", ("lat", "day"), None),
    )
    out_specs = (P("day", None, "lon", "lat"), P(None, "lon", ("lat", "day")))
    return jax.shard_map(
        functools.partial(on_device, mesh.shape["day"], mesh.shape["lon"]),
        mesh=mesh, in_specs=in_specs, out_specs=out_specs, check_vma=False,
    )
```

```python
import functools

import jax
import jax.numpy as jnp
from jax import lax
from jax.experimental import pallas as pl
from jax.experimental.pallas import tpu as pltpu
from jax.sharding import PartitionSpec as P

RIM = 3
SLOT = 8
F32 = jnp.float32
BF16 = jnp.bfloat16


def kernel(
    days, lons, runs_hbm, outlook_hbm, scale, obs_hbm, chosen_hbm, metric_out, prediction_out,
    runs, outlook, obs, chosen, metric_v, weights, load_sem,
    outlook_f, local, inner, cross, boxed, edge, edge_in, corner, corner_in, rim, rim_in,
    bits, bits_t, packed, mask_send, mask_in, part, part_send, part_in, flip,
    near_send, near_recv, mask_ssem, mask_rsem, part_ssem, part_rsem,
):
    variables, leads, cols, own_days, rows = runs.shape
    matches = chosen.shape[1]
    share = rows // days
    groups = -(-cols // days)
    per_tile = rows // SLOT
    day, lon, lat = lax.axis_index("day"), lax.axis_index("lon"), lax.axis_index("lat")
    left, right = lax.rem(lon + lons - 1, lons), lax.rem(lon + 1, lons)
    other = 1 - lat

    nearby = [
        {"lon": left}, {"lon": right},
        {"lon": left, "lat": other}, {"lon": right, "lat": other},
        {"lat": other},
    ]
    owners = [lax.rem(day + step, days) for step in range(days)]
    loads = [
        pltpu.make_async_copy(chosen_hbm, chosen, load_sem.at[3]),
        pltpu.make_async_copy(outlook_hbm, outlook, load_sem.at[0]),
        pltpu.make_async_copy(runs_hbm.at[:, :, :RIM], runs.at[:, :, :RIM], load_sem.at[1]),
        pltpu.make_async_copy(runs_hbm.at[:, :, cols - RIM:], runs.at[:, :, cols - RIM:], load_sem.at[2]),
        pltpu.make_async_copy(
            runs_hbm.at[:, :, RIM:cols - RIM], runs.at[:, :, RIM:cols - RIM], load_sem.at[4]),
        pltpu.make_async_copy(obs_hbm, obs, load_sem.at[5]),
    ]
    for load in loads:
        load.start()

    barrier = pltpu.get_barrier_semaphore()
    for device in nearby + [{"day": owner} for owner in owners[1:]]:
        pl.semaphore_signal(barrier, inc=1, device_id=device, device_id_type=pl.DeviceIdType.MESH)

    lane = lax.broadcasted_iota(jnp.int32, (own_days, rows), 1)
    slot_of = lane // SLOT
    part_of = lane // share

    def send(src, dst, ssem, rsem, device):
        copy = pltpu.make_async_remote_copy(
            src_ref=src, dst_ref=dst, send_sem=ssem, recv_sem=rsem,
            device_id=device, device_id_type=pl.DeviceIdType.MESH,
        )
        copy.start()
        return copy

    loads[0].wait()
    words = days * own_days // 32
    targets_per_word = 32 // own_days
    for t in range(bits.shape[0]):
        bits[t] = jnp.zeros((rows, rows), jnp.int32)
    for l in range(leads):
        sums = [jnp.zeros((share, cols), jnp.int32) for _ in range(words)]
        for k in range(matches):
            index = chosen[l, k]
            bit = lax.shift_left(jnp.ones_like(index), index & 31)
            word = lax.shift_right_logical(index, jnp.full_like(index, 5))
            for w in range(words):
                sums[w] = sums[w] | jnp.where(word == w, bit, 0)
        for w in range(words):
            c = w * leads + l
            at = (c % days) * share
            bits[c // days, at:at + share, :cols] = sums[w]
    for t in range(bits.shape[0]):
        bits_t[t] = bits[t].T
    group_lane = lax.broadcasted_iota(jnp.int32, (groups, rows), 1) // share
    for c in range(words * leads):
        total = jnp.zeros((groups, rows), jnp.int32)
        for i in range(days):
            moved = bits_t[c // days, pl.ds(i, groups, stride=days), :]
            shift = (share * (i - c % days)) % rows
            if shift:
                moved = pltpu.roll(moved, shift, 1)
            total = jnp.where(group_lane == i, moved, total)
        packed[c, :groups] = total

    day_row = lax.broadcasted_iota(jnp.int32, (own_days, rows), 0)

    def expand(owner, l, store):
        shift = day_row + lax.rem(owner, targets_per_word) * own_days
        base = (owner // targets_per_word) * leads

        @pl.loop(0, groups)
        def _(q):
            row = jnp.broadcast_to(packed[base + l, pl.ds(q, 1), :], (own_days, rows))
            store(q, (lax.shift_right_logical(row, shift) & 1).astype(F32).astype(BF16))

    masks = [[] for _ in range(leads)]

    def send_masks(l):
        for step in range(1, days):
            def store(q, value):
                mask_send[step - 1, l, q] = value
            expand(owners[step], l, store)
            masks[l].append(send(
                mask_send.at[step - 1, l], mask_in.at[day, l],
                mask_ssem.at[step - 1, l], mask_rsem.at[step - 1, l], {"day": owners[step]},
            ))

    pl.semaphore_wait(barrier, len(nearby) + days - 1)
    send_masks(0)
    loads[1].wait()
    for p in range(variables):
        for l in range(leads):
            outlook_f[p * leads + l] = outlook[p, l].astype(F32)

    def squares(l, x):
        total = jnp.zeros((own_days, rows), F32)
        for p in range(variables):
            diff = runs[p, l, x].astype(F32) - outlook_f[p * leads + l, pl.ds(x, 1), :]
            total = total + scale[p] * (diff * diff)
        return total.astype(BF16)

    def edge_columns(x, side):
        for l in range(leads):
            value = squares(l, x + side * (cols - RIM))
            local[l, x + side * (cols - RIM)] = value
            edge[side, l * RIM + x] = value

    for side in range(2):
        loads[2 + side].wait()

        @pl.loop(0, RIM)
        def _(x):
            edge_columns(x, side)
        total = jnp.zeros((own_days, rows), F32)
        for s in range(leads * RIM):
            moved = pltpu.roll(edge[side, s].astype(F32), RIM + SLOT * s, 1)
            total = jnp.where(slot_of == s, moved, total)
        corner[side] = total.astype(BF16)

    near = []
    for side, (device, across) in enumerate([(nearby[0], nearby[2]), (nearby[1], nearby[3])]):
        near.append(send(edge.at[side], edge_in.at[1 - side], near_send.at[side], near_recv.at[side], device))
        near.append(send(corner.at[side], corner_in.at[1 - side], near_send.at[2 + side], near_recv.at[2 + side], across))

    for l in range(1, leads - 1):
        send_masks(l)

    loads[4].wait()

    @pl.loop(RIM, cols - RIM)
    def _(x):
        for l in range(leads):
            local[l, x] = squares(l, x)

    @pl.loop(0, leads)
    def _(l):
        for g in range(rim.shape[1]):
            total = jnp.zeros((own_days, rows), F32)
            for s in range(min(per_tile, cols - g * per_tile)):
                tile = local[l, g * per_tile + s].astype(F32)
                total = jnp.where(slot_of == s, pltpu.roll(tile, (RIM + SLOT * s) % rows, 1), total)
            rim[l, g] = total.astype(BF16)

    near.append(send(rim, rim_in, near_send.at[4], near_recv.at[4], nearby[4]))

    send_masks(leads - 1)
    for l in range(leads):
        def own_store(q, value):
            mask_in[day, l, q] = value
        expand(owners[0], l, own_store)

    source = lax.broadcasted_iota(jnp.int32, (rows, rows), 0)
    target = lax.broadcasted_iota(jnp.int32, (rows, rows), 1)
    inner[...] = jnp.where(jnp.abs(source - target) <= RIM, 1.0, 0.0).astype(BF16)
    out_at, in_at = target % SLOT, source % SLOT
    row_out = jnp.where(out_at < RIM, rows - RIM + out_at, out_at - RIM)
    row_in = in_at - RIM + rows * other
    first = RIM * other
    cross[...] = jnp.where(
        (source // SLOT == target // SLOT) & (out_at < 2 * RIM) & (in_at >= first)
        & (in_at < first + RIM) & (jnp.abs(row_in - row_out) <= RIM), 1.0, 0.0).astype(BF16)
    part[...] = jnp.zeros(part.shape, F32)

    @pl.loop(0, leads)
    def _(l):
        product = jnp.dot(
            local[l].reshape(cols * own_days, rows), inner[...], preferred_element_type=F32)
        boxed[l, RIM:RIM + cols] = product.reshape(cols, own_days, rows)

    outer = (lane < RIM) | (lane >= rows - RIM)

    def unpacked(product, s):
        return jnp.where(outer, pltpu.roll(product, (rows - RIM - SLOT * s) % rows, 1), 0.0)

    for copy in near[:4]:
        copy.wait()
    for side in range(2):
        flat = edge_in[side].reshape(leads * RIM * own_days, rows)
        sides = jnp.dot(flat, inner[...], preferred_element_type=F32)
        sides = sides.reshape(leads * RIM, own_days, rows)
        product = jnp.dot(corner_in[side], cross[...], preferred_element_type=F32)
        for l in range(leads):
            for c in range(RIM):
                s = l * RIM + c
                boxed[l, side * (cols + RIM) + c] = sides[s] + unpacked(product, s)

    for copy in near[4:]:
        copy.wait()

    @pl.loop(0, leads)
    def _(l):
        for g in range(rim.shape[1]):
            product = jnp.dot(rim_in[l, g], cross[...], preferred_element_type=F32)
            for s in range(min(per_tile, cols - g * per_tile)):
                x = g * per_tile + s + RIM
                boxed[l, x] = boxed[l, x] + unpacked(product, s)

    def weigh(start, count):
        window = []
        for l in range(leads):
            y = [boxed[l, start + i] for i in range(count + 2 * RIM)]
            two = [y[i] + y[i + 1] for i in range(count + 5)]
            window.append([two[i] + two[i + 2] + (two[i + 4] + y[i + 6]) for i in range(count)])
        for l in range(leads):
            for i in range(count):
                total = window[l][i]
                if l > 0:
                    total = total + window[l - 1][i]
                if l < leads - 1:
                    total = total + window[l + 1][i]
                metric = total * (1.0 / 147.0)
                metric_v[l, start + i] = metric
                weights[l, start + i] = (1.0 / (metric + 1e-5)).astype(BF16)

    @pl.loop(0, cols // days)
    def _(q):
        weigh(q * days, days)
    if cols % days:
        weigh(cols - cols % days, cols % days)
    metric_copy = pltpu.make_async_copy(metric_v, metric_out, load_sem.at[6])
    metric_copy.start()

    loads[5].wait()

    def pick(l, q, count):
        masked = [mask_in[g, l, q].astype(F32) for g in range(days)]
        for i in range(count):
            x = q * days + i
            picked = jnp.zeros((own_days, rows), F32)
            for g in range(days):
                shift = (share * (g - i)) % rows
                moved = pltpu.roll(masked[g], shift, 1) if shift else masked[g]
                picked = jnp.where(part_of == g, moved, picked)
            weight = weights[l, x].astype(F32) * picked
            part[0, pl.ds(x, 1), :] = jnp.sum(weight * obs[l, x].astype(F32), axis=0, keepdims=True)
            part[1, pl.ds(x, 1), :] = jnp.sum(weight, axis=0, keepdims=True)

    half = part.shape[1] // 2
    half_part = lax.broadcasted_iota(jnp.int32, (half, rows), 1) // share
    partials = []
    for l in range(leads):
        for copy in masks[l]:
            copy.wait()

        @pl.loop(0, cols // days)
        def _(q):
            pick(l, q, days)
        if cols % days:
            pick(l, cols // days, cols % days)

        for step in [*range(1, days), 0]:
            total = jnp.zeros((half, rows), F32)
            for slot in range(4):
                shift = lax.rem(share * (slot - owners[step]) + rows * days, rows)
                at = half * (slot // 2)
                moved = pltpu.roll(part[slot % 2, at:at + half, :], shift, 1)
                total = jnp.where(half_part == slot, moved, total)
            if step:
                part_send[step - 1, l] = total
                partials.append(send(
                    part_send.at[step - 1, l], part_in.at[step, l],
                    part_ssem.at[step - 1, l], part_rsem.at[step - 1, l], {"day": owners[step]},
                ))
            else:
                part_in[0, l] = total
    flip[...] = jnp.zeros(flip.shape, F32)
    metric_copy.wait()
    for copy in partials:
        copy.wait()
    halves = [jnp.zeros((half, rows), F32) for _ in range(2)]
    for l in range(leads):
        total = part_in[0, l]
        for step in range(1, days):
            total = total + part_in[step, l]
        ratio = total / pltpu.roll(total, rows - share, 1)
        for h in range(2):
            shift = (share * (l - 2 * h)) % rows
            moved = pltpu.roll(ratio, shift, 1) if shift else ratio
            halves[h] = jnp.where(half_part == l, moved, halves[h])
    for h in range(2):
        flip[half * h:half * (h + 1)] = halves[h]
    turned = flip[...].T
    for l in range(leads):
        prediction_out[l] = turned[l * share:(l + 1) * share, :cols]


def hand_over(metric, prediction, metric_out, prediction_out, sem):
    leads, cols = metric.shape[:2]
    copies = [pltpu.make_async_copy(prediction, prediction_out, sem.at[2 * leads])]
    for l in range(leads):
        for h in range(2):
            part = pl.ds(h * (cols // 2), cols // 2 + h * (cols % 2))
            copies.append(pltpu.make_async_copy(
                metric.at[l, part], metric_out.at[l, part], sem.at[2 * l + h]))
    for copy in copies:
        copy.start()
    for copy in copies:
        copy.wait()


def on_device(days, lons, runs, outlook, scale, obs, chosen):
    runs = jnp.transpose(runs, (1, 2, 3, 0, 4))
    obs = jnp.transpose(obs, (1, 2, 0, 3))
    chosen = jnp.transpose(chosen, (0, 3, 2, 1))
    variables, leads, cols, own_days, rows = runs.shape
    share = rows // days
    groups = -(-cols // days)
    words = days * own_days // 32
    tiles = -(-words * leads // days)
    rims = -(-cols // (rows // SLOT))
    wide = -(-cols // 16) * 16
    tile = (own_days, rows)
    vmem = pl.BlockSpec(memory_space=pltpu.VMEM)
    hbm = pl.BlockSpec(memory_space=pltpu.HBM)
    metric, prediction = pl.pallas_call(
        functools.partial(kernel, days, lons),
        out_shape=(
            jax.ShapeDtypeStruct((leads, cols) + tile, F32),
            jax.ShapeDtypeStruct((leads, share, cols), F32),
        ),
        in_specs=[hbm, hbm, pl.BlockSpec(memory_space=pltpu.SMEM), hbm, hbm],
        out_specs=(hbm, vmem),
        scratch_shapes=[
            pltpu.VMEM(runs.shape, BF16),
            pltpu.VMEM(outlook.shape, BF16),
            pltpu.VMEM(obs.shape, BF16),
            pltpu.VMEM(chosen.shape, jnp.int32),
            pltpu.VMEM((leads, cols) + tile, F32),
            pltpu.VMEM((leads, cols) + tile, BF16),
            pltpu.SemaphoreType.DMA((7,)),
            pltpu.VMEM((variables * leads, cols, rows), F32),
            pltpu.VMEM((leads, cols) + tile, BF16),
            pltpu.VMEM((rows, rows), BF16),
            pltpu.VMEM((rows, rows), BF16),
            pltpu.VMEM((leads, cols + 2 * RIM) + tile, F32),
            pltpu.VMEM((2, leads * RIM) + tile, BF16),
            pltpu.VMEM((2, leads * RIM) + tile, BF16),
            pltpu.VMEM((2,) + tile, BF16),
            pltpu.VMEM((2,) + tile, BF16),
            pltpu.VMEM((leads, rims) + tile, BF16),
            pltpu.VMEM((leads, rims) + tile, BF16),
            pltpu.VMEM((tiles, rows, rows), jnp.int32),
            pltpu.VMEM((tiles, rows, rows), jnp.int32),
            pltpu.VMEM((words * leads, -(-groups // 8) * 8, rows), jnp.int32),
            pltpu.VMEM((days - 1, leads, groups) + tile, BF16),
            pltpu.VMEM((days, leads, groups) + tile, BF16),
            pltpu.VMEM((2, wide, rows), F32),
            pltpu.VMEM((days - 1, leads, wide // 2, rows), F32),
            pltpu.VMEM((days, leads, wide // 2, rows), F32),
            pltpu.VMEM((rows, rows), F32),
            pltpu.SemaphoreType.DMA((5,)),
            pltpu.SemaphoreType.DMA((5,)),
            pltpu.SemaphoreType.DMA((days - 1, leads)),
            pltpu.SemaphoreType.DMA((days - 1, leads)),
            pltpu.SemaphoreType.DMA((days - 1, leads)),
            pltpu.SemaphoreType.DMA((days - 1, leads)),
        ],
        compiler_params=pltpu.CompilerParams(
            collective_id=0, has_side_effects=True, vmem_limit_bytes=64 * 2**20 - 2**16
        ),
    )(runs, outlook, scale, obs, chosen)
    metric, prediction = pl.pallas_call(
        hand_over,
        out_shape=(
            jax.ShapeDtypeStruct(metric.shape, F32),
            jax.ShapeDtypeStruct(prediction.shape, F32),
        ),
        in_specs=[hbm, hbm],
        out_specs=(hbm, hbm),
        scratch_shapes=[pltpu.SemaphoreType.DMA((2 * leads + 1,))],
        compiler_params=pltpu.CompilerParams(vmem_limit_bytes=64 * 2**20 - 2**16),
    )(metric, prediction)
    return jnp.transpose(metric, (2, 0, 1, 3)), jnp.transpose(prediction, (0, 2, 1))


def solution(mesh):
    in_specs = (
        P("day", None, None, "lon", "lat"),
        P(None, None, "lon", "lat"),
        P(),
        P("day", None, "lon", "lat"),
        P(None, "lon", ("lat", "day"), None),
    )
    out_specs = (P("day", None, "lon", "lat"), P(None, "lon", ("lat", "day")))
    return jax.shard_map(
        functools.partial(on_device, mesh.shape["day"], mesh.shape["lon"]),
        mesh=mesh, in_specs=in_specs, out_specs=out_specs, check_vma=False,
    )
```

```python
import functools

import jax
import jax.numpy as jnp
from jax import lax
from jax.experimental import pallas as pl
from jax.experimental.pallas import tpu as pltpu
from jax.sharding import PartitionSpec as P

RIM = 3
SLOT = 8
F32 = jnp.float32
BF16 = jnp.bfloat16


def kernel(
    days, lons, runs_hbm, outlook_hbm, scale, obs_hbm, chosen_hbm, metric_out, prediction_out,
    runs, outlook, obs, chosen, metric_v, weights, load_sem,
    outlook_f, local, inner, cross, boxed, edge, edge_in, corner, corner_in, rim, rim_in,
    bits, bits_t, packed, mask_send, mask_in, part, part_send, part_in, flip,
    near_send, near_recv, mask_ssem, mask_rsem, part_ssem, part_rsem,
):
    variables, leads, cols, own_days, rows = runs.shape
    matches = chosen.shape[1]
    share = rows // days
    groups = -(-cols // days)
    per_tile = rows // SLOT
    day, lon, lat = lax.axis_index("day"), lax.axis_index("lon"), lax.axis_index("lat")
    left, right = lax.rem(lon + lons - 1, lons), lax.rem(lon + 1, lons)
    other = 1 - lat

    nearby = [
        {"lon": left}, {"lon": right},
        {"lon": left, "lat": other}, {"lon": right, "lat": other},
        {"lat": other},
    ]
    owners = [lax.rem(day + step, days) for step in range(days)]
    loads = [
        pltpu.make_async_copy(chosen_hbm, chosen, load_sem.at[3]),
        pltpu.make_async_copy(outlook_hbm, outlook, load_sem.at[0]),
        pltpu.make_async_copy(runs_hbm.at[:, :, :RIM], runs.at[:, :, :RIM], load_sem.at[1]),
        pltpu.make_async_copy(runs_hbm.at[:, :, cols - RIM:], runs.at[:, :, cols - RIM:], load_sem.at[2]),
        pltpu.make_async_copy(
            runs_hbm.at[:, :, RIM:cols - RIM], runs.at[:, :, RIM:cols - RIM], load_sem.at[4]),
        pltpu.make_async_copy(obs_hbm, obs, load_sem.at[5]),
    ]
    for load in loads:
        load.start()

    barrier = pltpu.get_barrier_semaphore()
    for device in nearby + [{"day": owner} for owner in owners[1:]]:
        pl.semaphore_signal(barrier, inc=1, device_id=device, device_id_type=pl.DeviceIdType.MESH)

    lane = lax.broadcasted_iota(jnp.int32, (own_days, rows), 1)
    slot_of = lane // SLOT
    part_of = lane // share

    def send(src, dst, ssem, rsem, device):
        copy = pltpu.make_async_remote_copy(
            src_ref=src, dst_ref=dst, send_sem=ssem, recv_sem=rsem,
            device_id=device, device_id_type=pl.DeviceIdType.MESH,
        )
        copy.start()
        return copy

    loads[0].wait()
    words = days * own_days // 32
    targets_per_word = 32 // own_days
    for t in range(bits.shape[0]):
        bits[t] = jnp.zeros((rows, rows), jnp.int32)
    for l in range(leads):
        sums = [jnp.zeros((share, cols), jnp.int32) for _ in range(words)]
        for k in range(matches):
            index = chosen[l, k]
            bit = lax.shift_left(jnp.ones_like(index), index & 31)
            word = lax.shift_right_logical(index, jnp.full_like(index, 5))
            for w in range(words):
                sums[w] = sums[w] | jnp.where(word == w, bit, 0)
        for w in range(words):
            c = w * leads + l
            at = (c % days) * share
            bits[c // days, at:at + share, :cols] = sums[w]
    for t in range(bits.shape[0]):
        bits_t[t] = bits[t].T
    group_lane = lax.broadcasted_iota(jnp.int32, (groups, rows), 1) // share
    for c in range(words * leads):
        total = jnp.zeros((groups, rows), jnp.int32)
        for i in range(days):
            moved = bits_t[c // days, pl.ds(i, groups, stride=days), :]
            shift = (share * (i - c % days)) % rows
            if shift:
                moved = pltpu.roll(moved, shift, 1)
            total = jnp.where(group_lane == i, moved, total)
        packed[c, :groups] = total

    day_row = lax.broadcasted_iota(jnp.int32, (own_days, rows), 0)

    def expand(owner, l, store):
        shift = day_row + lax.rem(owner, targets_per_word) * own_days
        base = (owner // targets_per_word) * leads

        @pl.loop(0, groups)
        def _(q):
            row = jnp.broadcast_to(packed[base + l, pl.ds(q, 1), :], (own_days, rows))
            store(q, (lax.shift_right_logical(row, shift) & 1).astype(F32).astype(BF16))

    masks = [[] for _ in range(leads)]

    def send_masks(l):
        for step in range(1, days):
            def store(q, value):
                mask_send[step - 1, l, q] = value
            expand(owners[step], l, store)
            masks[l].append(send(
                mask_send.at[step - 1, l], mask_in.at[day, l],
                mask_ssem.at[step - 1, l], mask_rsem.at[step - 1, l], {"day": owners[step]},
            ))

    pl.semaphore_wait(barrier, len(nearby) + days - 1)
    send_masks(0)
    loads[1].wait()
    for p in range(variables):
        for l in range(leads):
            outlook_f[p * leads + l] = outlook[p, l].astype(F32)

    def squares(l, x):
        total = jnp.zeros((own_days, rows), F32)
        for p in range(variables):
            diff = runs[p, l, x].astype(F32) - outlook_f[p * leads + l, pl.ds(x, 1), :]
            total = total + scale[p] * (diff * diff)
        return total.astype(BF16)

    def edge_columns(x, side):
        for l in range(leads):
            value = squares(l, x + side * (cols - RIM))
            local[l, x + side * (cols - RIM)] = value
            edge[side, l * RIM + x] = value

    for side in range(2):
        loads[2 + side].wait()

        @pl.loop(0, RIM)
        def _(x):
            edge_columns(x, side)
        total = jnp.zeros((own_days, rows), F32)
        for s in range(leads * RIM):
            moved = pltpu.roll(edge[side, s].astype(F32), RIM + SLOT * s, 1)
            total = jnp.where(slot_of == s, moved, total)
        corner[side] = total.astype(BF16)

    near = []
    for side, (device, across) in enumerate([(nearby[0], nearby[2]), (nearby[1], nearby[3])]):
        near.append(send(edge.at[side], edge_in.at[1 - side], near_send.at[side], near_recv.at[side], device))
        near.append(send(corner.at[side], corner_in.at[1 - side], near_send.at[2 + side], near_recv.at[2 + side], across))

    for l in range(1, leads - 1):
        send_masks(l)

    loads[4].wait()

    @pl.loop(RIM, cols - RIM)
    def _(x):
        for l in range(leads):
            local[l, x] = squares(l, x)

    @pl.loop(0, leads)
    def _(l):
        for g in range(rim.shape[1]):
            total = jnp.zeros((own_days, rows), F32)
            for s in range(min(per_tile, cols - g * per_tile)):
                tile = local[l, g * per_tile + s].astype(F32)
                total = jnp.where(slot_of == s, pltpu.roll(tile, (RIM + SLOT * s) % rows, 1), total)
            rim[l, g] = total.astype(BF16)

    near.append(send(rim, rim_in, near_send.at[4], near_recv.at[4], nearby[4]))

    send_masks(leads - 1)
    for l in range(leads):
        def own_store(q, value):
            mask_in[day, l, q] = value
        expand(owners[0], l, own_store)

    source = lax.broadcasted_iota(jnp.int32, (rows, rows), 0)
    target = lax.broadcasted_iota(jnp.int32, (rows, rows), 1)
    inner[...] = jnp.where(jnp.abs(source - target) <= RIM, 1.0, 0.0).astype(BF16)
    out_at, in_at = target % SLOT, source % SLOT
    row_out = jnp.where(out_at < RIM, rows - RIM + out_at, out_at - RIM)
    row_in = in_at - RIM + rows * other
    first = RIM * other
    cross[...] = jnp.where(
        (source // SLOT == target // SLOT) & (out_at < 2 * RIM) & (in_at >= first)
        & (in_at < first + RIM) & (jnp.abs(row_in - row_out) <= RIM), 1.0, 0.0).astype(BF16)
    part[...] = jnp.zeros(part.shape, F32)

    @pl.loop(0, leads)
    def _(l):
        product = jnp.dot(
            local[l].reshape(cols * own_days, rows), inner[...], preferred_element_type=F32)
        boxed[l, RIM:RIM + cols] = product.reshape(cols, own_days, rows)

    outer = (lane < RIM) | (lane >= rows - RIM)

    def unpacked(product, s):
        return jnp.where(outer, pltpu.roll(product, (rows - RIM - SLOT * s) % rows, 1), 0.0)

    for copy in near[:4]:
        copy.wait()
    for side in range(2):
        flat = edge_in[side].reshape(leads * RIM * own_days, rows)
        sides = jnp.dot(flat, inner[...], preferred_element_type=F32)
        sides = sides.reshape(leads * RIM, own_days, rows)
        product = jnp.dot(corner_in[side], cross[...], preferred_element_type=F32)
        for l in range(leads):
            for c in range(RIM):
                s = l * RIM + c
                boxed[l, side * (cols + RIM) + c] = sides[s] + unpacked(product, s)

    for copy in near[4:]:
        copy.wait()

    @pl.loop(0, leads)
    def _(l):
        for g in range(rim.shape[1]):
            product = jnp.dot(rim_in[l, g], cross[...], preferred_element_type=F32)
            for s in range(min(per_tile, cols - g * per_tile)):
                x = g * per_tile + s + RIM
                boxed[l, x] = boxed[l, x] + unpacked(product, s)

    def weigh(start, count):
        window = []
        for l in range(leads):
            y = [boxed[l, start + i] for i in range(count + 2 * RIM)]
            two = [y[i] + y[i + 1] for i in range(count + 5)]
            window.append([two[i] + two[i + 2] + (two[i + 4] + y[i + 6]) for i in range(count)])
        for l in range(leads):
            for i in range(count):
                total = window[l][i]
                if l > 0:
                    total = total + window[l - 1][i]
                if l < leads - 1:
                    total = total + window[l + 1][i]
                metric = total * (1.0 / 147.0)
                metric_v[l, start + i] = metric
                weights[l, start + i] = (1.0 / (metric + 1e-5)).astype(BF16)

    @pl.loop(0, cols // days)
    def _(q):
        weigh(q * days, days)
    if cols % days:
        weigh(cols - cols % days, cols % days)
    metric_copy = pltpu.make_async_copy(metric_v, metric_out, load_sem.at[6])
    metric_copy.start()

    loads[5].wait()

    def pick(l, q, count):
        masked = [mask_in[g, l, q].astype(F32) for g in range(days)]
        for i in range(count):
            x = q * days + i
            picked = jnp.zeros((own_days, rows), F32)
            for g in range(days):
                shift = (share * (g - i)) % rows
                moved = pltpu.roll(masked[g], shift, 1) if shift else masked[g]
                picked = jnp.where(part_of == g, moved, picked)
            weight = weights[l, x].astype(F32) * picked
            part[0, pl.ds(x, 1), :] = jnp.sum(weight * obs[l, x].astype(F32), axis=0, keepdims=True)
            part[1, pl.ds(x, 1), :] = jnp.sum(weight, axis=0, keepdims=True)

    half = part.shape[1] // 2
    half_part = lax.broadcasted_iota(jnp.int32, (half, rows), 1) // share
    partials = []
    for l in range(leads):
        for copy in masks[l]:
            copy.wait()

        @pl.loop(0, cols // days)
        def _(q):
            pick(l, q, days)
        if cols % days:
            pick(l, cols // days, cols % days)

        for step in [*range(1, days), 0]:
            total = jnp.zeros((half, rows), F32)
            for slot in range(4):
                shift = lax.rem(share * (slot - owners[step]) + rows * days, rows)
                at = half * (slot // 2)
                moved = pltpu.roll(part[slot % 2, at:at + half, :], shift, 1)
                total = jnp.where(half_part == slot, moved, total)
            if step:
                part_send[step - 1, l] = total
                partials.append(send(
                    part_send.at[step - 1, l], part_in.at[step, l],
                    part_ssem.at[step - 1, l], part_rsem.at[step - 1, l], {"day": owners[step]},
                ))
            else:
                part_in[0, l] = total
    flip[...] = jnp.zeros(flip.shape, F32)
    metric_copy.wait()
    for copy in partials:
        copy.wait()
    halves = [jnp.zeros((half, rows), F32) for _ in range(2)]
    for l in range(leads):
        total = part_in[0, l]
        for step in range(1, days):
            total = total + part_in[step, l]
        ratio = total / pltpu.roll(total, rows - share, 1)
        for h in range(2):
            shift = (share * (l - 2 * h)) % rows
            moved = pltpu.roll(ratio, shift, 1) if shift else ratio
            halves[h] = jnp.where(half_part == l, moved, halves[h])
    for h in range(2):
        flip[half * h:half * (h + 1)] = halves[h]
    turned = flip[...].T
    for l in range(leads):
        prediction_out[l] = turned[l * share:(l + 1) * share, :cols]


def hand_over(metric, prediction, metric_out, prediction_out, metric_v, prediction_v, sem):
    leads, cols = metric.shape[:2]
    pieces = [(prediction, prediction_v, prediction_out)]
    for l in range(leads):
        for h in range(2):
            at = (l, pl.ds(h * (cols // 2), cols // 2 + h * (cols % 2)))
            pieces.append((metric.at[at], metric_v.at[at], metric_out.at[at]))
    loads = [pltpu.make_async_copy(src, mid, sem.at[0, i]) for i, (src, mid, _) in enumerate(pieces)]
    stores = [pltpu.make_async_copy(mid, dst, sem.at[1, i]) for i, (_, mid, dst) in enumerate(pieces)]
    for load in loads:
        load.start()
    for load, store in zip(loads, stores):
        load.wait()
        store.start()
    for store in stores:
        store.wait()


def on_device(days, lons, runs, outlook, scale, obs, chosen):
    runs = jnp.transpose(runs, (1, 2, 3, 0, 4))
    obs = jnp.transpose(obs, (1, 2, 0, 3))
    chosen = jnp.transpose(chosen, (0, 3, 2, 1))
    variables, leads, cols, own_days, rows = runs.shape
    share = rows // days
    groups = -(-cols // days)
    words = days * own_days // 32
    tiles = -(-words * leads // days)
    rims = -(-cols // (rows // SLOT))
    wide = -(-cols // 16) * 16
    tile = (own_days, rows)
    vmem = pl.BlockSpec(memory_space=pltpu.VMEM)
    hbm = pl.BlockSpec(memory_space=pltpu.HBM)
    metric, prediction = pl.pallas_call(
        functools.partial(kernel, days, lons),
        out_shape=(
            jax.ShapeDtypeStruct((leads, cols) + tile, F32),
            jax.ShapeDtypeStruct((leads, share, cols), F32),
        ),
        in_specs=[hbm, hbm, pl.BlockSpec(memory_space=pltpu.SMEM), hbm, hbm],
        out_specs=(hbm, vmem),
        scratch_shapes=[
            pltpu.VMEM(runs.shape, BF16),
            pltpu.VMEM(outlook.shape, BF16),
            pltpu.VMEM(obs.shape, BF16),
            pltpu.VMEM(chosen.shape, jnp.int32),
            pltpu.VMEM((leads, cols) + tile, F32),
            pltpu.VMEM((leads, cols) + tile, BF16),
            pltpu.SemaphoreType.DMA((7,)),
            pltpu.VMEM((variables * leads, cols, rows), F32),
            pltpu.VMEM((leads, cols) + tile, BF16),
            pltpu.VMEM((rows, rows), BF16),
            pltpu.VMEM((rows, rows), BF16),
            pltpu.VMEM((leads, cols + 2 * RIM) + tile, F32),
            pltpu.VMEM((2, leads * RIM) + tile, BF16),
            pltpu.VMEM((2, leads * RIM) + tile, BF16),
            pltpu.VMEM((2,) + tile, BF16),
            pltpu.VMEM((2,) + tile, BF16),
            pltpu.VMEM((leads, rims) + tile, BF16),
            pltpu.VMEM((leads, rims) + tile, BF16),
            pltpu.VMEM((tiles, rows, rows), jnp.int32),
            pltpu.VMEM((tiles, rows, rows), jnp.int32),
            pltpu.VMEM((words * leads, -(-groups // 8) * 8, rows), jnp.int32),
            pltpu.VMEM((days - 1, leads, groups) + tile, BF16),
            pltpu.VMEM((days, leads, groups) + tile, BF16),
            pltpu.VMEM((2, wide, rows), F32),
            pltpu.VMEM((days - 1, leads, wide // 2, rows), F32),
            pltpu.VMEM((days, leads, wide // 2, rows), F32),
            pltpu.VMEM((rows, rows), F32),
            pltpu.SemaphoreType.DMA((5,)),
            pltpu.SemaphoreType.DMA((5,)),
            pltpu.SemaphoreType.DMA((days - 1, leads)),
            pltpu.SemaphoreType.DMA((days - 1, leads)),
            pltpu.SemaphoreType.DMA((days - 1, leads)),
            pltpu.SemaphoreType.DMA((days - 1, leads)),
        ],
        compiler_params=pltpu.CompilerParams(
            collective_id=0, has_side_effects=True, vmem_limit_bytes=64 * 2**20 - 2**16
        ),
    )(runs, outlook, scale, obs, chosen)
    metric, prediction = pl.pallas_call(
        hand_over,
        out_shape=(
            jax.ShapeDtypeStruct(metric.shape, F32),
            jax.ShapeDtypeStruct(prediction.shape, F32),
        ),
        in_specs=[hbm, hbm],
        out_specs=(hbm, hbm),
        scratch_shapes=[
            pltpu.VMEM(metric.shape, F32),
            pltpu.VMEM(prediction.shape, F32),
            pltpu.SemaphoreType.DMA((2, 2 * leads + 1)),
        ],
        compiler_params=pltpu.CompilerParams(vmem_limit_bytes=64 * 2**20 - 2**16),
    )(metric, prediction)
    return jnp.transpose(metric, (2, 0, 1, 3)), jnp.transpose(prediction, (0, 2, 1))


def solution(mesh):
    in_specs = (
        P("day", None, None, "lon", "lat"),
        P(None, None, "lon", "lat"),
        P(),
        P("day", None, "lon", "lat"),
        P(None, "lon", ("lat", "day"), None),
    )
    out_specs = (P("day", None, "lon", "lat"), P(None, "lon", ("lat", "day")))
    return jax.shard_map(
        functools.partial(on_device, mesh.shape["day"], mesh.shape["lon"]),
        mesh=mesh, in_specs=in_specs, out_specs=out_specs, check_vma=False,
    )
```
